32 devices in a mesh: row: 4 (over x, core), col: 8 (over z, y).
Axes of the slice: x: 2, y: 2, z: 4, core: 2. Of those that a mesh axis runs over, the one named last changes fastest.
Arguments:
- tokens: bfloat16 [12288, 2048], P('col', 'row'), may hold values from -6 to 6
- in_weight: float32 [2048, 6144], P(('row', 'col')), may hold values from -0.125 to 0.125
- out_weight: float32 [2048, 2048], P(('row', 'col')), may hold values from -0.125 to 0.125
- beta_weight: float32 [2048, 16], replicated, may hold values from -0.25 to 0.25
- conv_weight: float32 [4, 6144], P(None, 'row'), may hold values from -2.5 to 2.5
- conv_prior: bfloat16 [24, 3, 6144], P('col', None, 'row'), may hold values from -6 to 6
- head_gain: float32 [2048], P('row'), may hold values from 0.1 to 1.9
- state_pool: float32 [48, 16, 128, 128], P('col', 'row'), may hold values from -2.5 to 2.5
- state_index: int32 [24, 16], P('col', 'row'), may hold values from 0 to 5
- lengths: int32 [24], P('col'), may hold values from 1 to 512, 9216 in all
- page_table: int32 [24, 4, 2], P('col'), may hold values from 0 to 11, as said below
Outputs:
- server_in: bfloat16 [2048, 6144], P('row', 'col')
- server_out: bfloat16 [2048, 2048], P('row', 'col')
- layer_out: bfloat16 [12288, 2048], P('col', 'row')
- final_state: float32 [24, 16, 128, 128], P('col', 'row')
- page_cache: bfloat16 [96, 128, 2, 2048], P('col', None, None, 'row')
The draws below stay inside these ranges and needn't reach their ends.
Inputs may be any that keep to these rules, and one draw needn't show every extreme that they name: `lengths`: one prompt has all 512 tokens live. `state_index`: which of its own index of col's 6 stored states a prompt and head continues. page_table[p, g, 0] is the index of col that keeps page g of prompt p and page_table[p, g, 1] its slot there, below 12; every slot of every index of col gets exactly one page; the prompts of one index of col send at most 3 pages to any one index of col, and exactly 3 to some.
All inputs are finite; a program needn't handle non-finite values. No bound on the sum of `lengths` on one device may be relied on, other than what follows from the above.
Results may differ from the reference program's by a relative error of at most 0.029.
Values may be sent and summed in bfloat16 or wider, within the bound.
A program may use at most 128 MiB of HBM per device.

```python
import math
import jax
import jax.numpy as jnp
import numpy as np
from jax import lax

D = 2048
HEADS = 16
DK = 128
STRETCH = 64
CONV = 4
SEQ = 512
PAGE = 128
PR_DEV = 3
PROMPTS = 24
TOKENS = 12288
QKV = 6144
HD = 2048
PAGES_SEQ = 4
PAGES_DEV = 12
CAP = 3
POOL_DEV = 6
N_ROW = 4
N_COL = 8


def draw_page_table(key, part):
    offset = jax.random.randint(jax.random.fold_in(key, 7), (), 0, N_COL)
    subkeys = jax.random.split(jax.random.fold_in(key, 11), N_COL)
    ranking = jax.vmap(lambda subkey: jax.random.permutation(subkey, PAGES_DEV))(subkeys).astype(jnp.int32)
    source = jnp.arange(N_COL, dtype=jnp.int32)[:, None]
    target = (source + ranking // CAP + offset) % N_COL
    entries = jnp.stack([target, ranking], axis=-1).astype(jnp.int32)
    return entries.reshape(PROMPTS, PAGES_SEQ, 2)


def touch_ends(values, key, smallest, largest):
    shape = values.shape
    spot = [jax.random.randint(jax.random.fold_in(key, axis), (), 0, shape[axis]) for axis in range(len(shape))]
    values = values.at[tuple(spot)].set(smallest)
    longest = shape.index(max(shape))
    spot[longest] = (spot[longest] + 1) % shape[longest]
    return values.at[tuple(spot)].set(largest)


def block_scale(own_key, shape, shards, low, largest):
    level = 1.0
    for position, blocks in shards:
        steps = jax.random.uniform(jax.random.fold_in(jax.random.fold_in(own_key, 6), position), (blocks,), jnp.float32, low / len(shards), largest / len(shards))
        level = level * jnp.repeat(jnp.exp(steps), shape[position] // blocks).reshape((-1,) + (1,) * (len(shape) - 1 - position))
    return level


def length_profile(amount, total, reach, slope):
    portions = [(1 << 20) // math.isqrt(rank ** slope) + 1 for rank in range(2, amount + 1)]
    spare, given = total - reach - (amount - 1), [1] * (amount - 1)
    while spare > 0:
        movable = [i for i in range(amount - 1) if given[i] < reach]
        whole, budget = sum([portions[i] for i in movable]), spare
        for i in movable:
            more = min(reach - given[i], max(1, budget * portions[i] // whole), spare)
            given[i] = given[i] + more
            spare = spare - more
    return np.array([reach] + given)


def ragged(key, count, total, reach, skew):
    if count == 2:
        one = jax.random.randint(key, (), max(1, total - reach), min(reach, total - 1) + 1)
        return jnp.stack([one, total - one])
    sizes = jnp.asarray(length_profile(count, total, reach, skew), jnp.int32)
    pairs = (count - 1) // 2
    donor, taker = sizes[1:1 + 2 * pairs:2], sizes[2:2 + 2 * pairs:2]
    margin = jnp.minimum(donor - 1, reach - taker)
    shifted = jax.random.randint(jax.random.fold_in(key, 1), (pairs,), 0, 1 << 20) % (margin + 1)
    sizes = sizes.at[1:1 + 2 * pairs:2].set(donor - shifted).at[2:2 + 2 * pairs:2].set(taker + shifted)
    return sizes[jax.random.permutation(jax.random.fold_in(key, 2), count)]


def scatter_about(rng, dims, width, bound, pieces=(), kind=jnp.bfloat16):
    loudness = block_scale(rng, dims, pieces, -0.22, 0.18) if pieces else 1.0
    array = jax.random.normal(rng, dims, jnp.float32) * width * loudness
    return jnp.minimum(jnp.maximum(array, -bound), bound).astype(kind)


def setup_inputs(seed: int = 0) -> dict:
    splits = jax.random.split(jax.random.key(seed), 12)
    tokens = scatter_about(splits[0], (TOKENS, D), 1.0, 6.0, ((0, 8), (1, 4)))
    in_weight = scatter_about(splits[1], (D, QKV), D ** -0.5, 0.125, ((0, 32),), jnp.float32)
    out_weight = scatter_about(splits[2], (HD, D), HD ** -0.5, 0.125, ((0, 32),), jnp.float32)
    beta_weight = scatter_about(splits[3], (D, HEADS), (D // 4) ** -0.5, 0.25, (), jnp.float32)
    conv_weight = scatter_about(splits[4], (CONV, QKV), 0.5, 2.5, ((1, 4),), jnp.float32)
    conv_prior = scatter_about(splits[5], (PROMPTS, CONV - 1, QKV), 1.0, 6.0, ((0, 8), (2, 4)))
    head_gain = jnp.clip(1.0 + 0.18 * jax.random.normal(splits[6], (HD,), jnp.float32), 0.1, 1.9)
    state_pool = scatter_about(splits[7], (N_COL * POOL_DEV, HEADS, DK, DK), 0.25, 2.5, ((0, 8), (1, 4)), jnp.float32)
    state_index = touch_ends(jax.random.randint(splits[8], (PROMPTS, HEADS), 0, POOL_DEV), jax.random.fold_in(splits[8], 1), 0, POOL_DEV - 1).astype(jnp.int32)
    lengths = ragged(splits[9], PROMPTS, PROMPTS * SEQ * 3 // 4, SEQ, 2).astype(jnp.int32)
    page_table = draw_page_table(jax.random.fold_in(splits[11], 71), 0)
    return {"tokens": tokens, "in_weight": in_weight, "out_weight": out_weight, "beta_weight": beta_weight, "conv_weight": conv_weight, "conv_prior": conv_prior, "head_gain": head_gain, "state_pool": state_pool, "state_index": state_index, "lengths": lengths, "page_table": page_table}


HIGHEST = lax.Precision.HIGHEST

def delta_block(carry_state, block_data):
    query_unit, key_unit, values, beta_rates = block_data
    width_c = beta_rates.shape[1]
    width_k = key_unit.shape[2]
    strict_lower = jnp.tril(jnp.ones((width_c, width_c), jnp.float32), -1)
    causal = jnp.tril(jnp.ones((width_c, width_c), jnp.float32))
    gram_matrix = jnp.einsum('bik,bjk->bij', key_unit, key_unit, precision=HIGHEST)
    system = jnp.eye(width_c, dtype=jnp.float32) + beta_rates[:, :, None] * gram_matrix * strict_lower
    right_side = jnp.concatenate([key_unit, values], axis=2) * beta_rates[:, :, None]
    solved = jax.scipy.linalg.solve_triangular(system, right_side, lower=True, unit_diagonal=True)
    weighted = solved[:, :, :width_k]
    corrected = solved[:, :, width_k:] - jnp.einsum('bck,bkv->bcv', weighted, carry_state, precision=HIGHEST)
    scores = jnp.einsum('bik,bjk->bij', query_unit, key_unit, precision=HIGHEST) * causal
    output = jnp.einsum('bck,bkv->bcv', query_unit, carry_state, precision=HIGHEST) + jnp.einsum('bij,bjv->biv', scores, corrected, precision=HIGHEST)
    carry_state = carry_state + jnp.einsum('bck,bcv->bkv', key_unit, corrected, precision=HIGHEST)
    return (carry_state, output)

def delta_scan(query_unit, key_unit, values, beta_rates, initial, block_len):
    batch_n = query_unit.shape[0]
    length_all = query_unit.shape[1]
    num_blocks = length_all // block_len

    def to_blocks(tensor):
        shaped = tensor.reshape((batch_n, num_blocks, block_len) + tensor.shape[2:])
        return jnp.moveaxis(shaped, 1, 0)
    last_state, outputs = lax.scan(delta_block, initial, (to_blocks(query_unit), to_blocks(key_unit), to_blocks(values), to_blocks(beta_rates)))
    outputs = jnp.moveaxis(outputs, 0, 1).reshape(batch_n, length_all, -1)
    return (last_state, outputs)

def unit_rows(tensor):
    return tensor * lax.rsqrt(lax.optimization_barrier(jnp.sum(tensor * tensor, axis=-1, keepdims=True)) + 1e-06)

def blockwise_product(left, right, groups):
    span_rows = left.shape[1] // groups
    running = jnp.zeros((left.shape[0], right.shape[1]), jnp.float32)
    for group_id in range(groups):
        piece_sum = jnp.dot(left[:, group_id * span_rows:(group_id + 1) * span_rows].astype(jnp.float32), right[group_id * span_rows:(group_id + 1) * span_rows].astype(jnp.float32), preferred_element_type=jnp.float32).astype(jnp.bfloat16)
        running = running + lax.optimization_barrier(piece_sum).astype(jnp.float32)
    return running.astype(jnp.bfloat16)

def reference(tokens, in_weight, out_weight, beta_weight, conv_weight, conv_prior, head_gain, state_pool, state_index, lengths, page_table):
    server_in = in_weight.astype(jnp.bfloat16)
    server_out = out_weight.astype(jnp.bfloat16)
    beta_cast = beta_weight.astype(jnp.bfloat16)
    prompt_ids = jnp.arange(PROMPTS, dtype=jnp.int32)
    pool_rows = (prompt_ids // PR_DEV * POOL_DEV)[:, None] + state_index
    initial = state_pool[pool_rows, jnp.arange(HEADS, dtype=jnp.int32)[None, :]]

    def prompt_layer(inputs):
        prompt_tokens, prior_rows, live_len, start_state = inputs
        live_mask = (jnp.arange(SEQ, dtype=jnp.int32) < live_len).astype(jnp.float32)
        projected = blockwise_product(prompt_tokens, server_in, N_ROW)
        beta_rates = live_mask[:, None] * jax.nn.sigmoid(jnp.dot(prompt_tokens.astype(jnp.float32), beta_cast.astype(jnp.float32), preferred_element_type=jnp.float32))
        padded = jnp.concatenate([prior_rows.astype(jnp.float32), projected.astype(jnp.float32)], axis=0)
        conv_sum = jnp.zeros((SEQ, QKV), jnp.float32)
        for tap_id in range(CONV):
            conv_sum = conv_sum + conv_weight[tap_id][None, :] * padded[tap_id:tap_id + SEQ]
        activated = jax.nn.silu(conv_sum).reshape(SEQ, HEADS, 3, DK).transpose(1, 2, 0, 3)
        query_unit = unit_rows(activated[:, 0])
        key_unit = unit_rows(activated[:, 1])
        values = activated[:, 2]
        last_state, outputs = delta_scan(query_unit, key_unit, values, beta_rates.T, start_state, STRETCH)
        outputs = outputs * live_mask[None, :, None]
        normed = outputs * lax.rsqrt(lax.optimization_barrier(jnp.mean(outputs * outputs, axis=2, keepdims=True)) + 1e-05) * head_gain.reshape(HEADS, 1, DK)
        normed = normed.astype(jnp.bfloat16).transpose(1, 0, 2).reshape(SEQ, HD)
        mixed_rows = blockwise_product(normed, server_out, N_ROW)
        keep_mask = live_mask[None, :, None]
        kept_pairs = jnp.stack([key_unit * keep_mask, values * keep_mask], axis=0)
        page_rows = kept_pairs.transpose(2, 0, 1, 3).reshape(PAGES_SEQ, PAGE, 2, HD).astype(jnp.bfloat16)
        return (mixed_rows, last_state, page_rows)
    mixed_all, state_all, page_all = lax.map(prompt_layer, (tokens.reshape(PROMPTS, SEQ, D), conv_prior, lengths, initial))
    targets = (page_table[:, :, 0] * PAGES_DEV + page_table[:, :, 1]).reshape(-1)
    page_cache = jnp.zeros((N_COL * PAGES_DEV, PAGE, 2, HD), jnp.bfloat16).at[targets].set(page_all.reshape(PROMPTS * PAGES_SEQ, PAGE, 2, HD))
    return (server_in, server_out, mixed_all.reshape(TOKENS, D), state_all, page_cache)
```

```python
import functools

import jax
import jax.numpy as jnp
from jax import lax
from jax.experimental import pallas as pl
from jax.experimental.pallas import tpu as pltpu
from jax.sharding import PartitionSpec as P

DK = 128
CONV = 4
SEQ = 512
PAGE = 128
PAGES_SEQ = 4
BF = jnp.bfloat16
F32 = jnp.float32
VMEM_LIMIT = 48 * 1024 * 1024


def project_kernel(
    lens, spots, tok, win, wbeta, taps, prior, q_out, k_out, v_out, rates_out, outgoing, line, kv, features, weights, sems
):
    prompt, head = pl.program_id(0), pl.program_id(1)
    heads = pl.num_programs(1)
    rows = tok.shape[0]
    span = tok.shape[2]
    live = lax.broadcasted_iota(jnp.int32, (SEQ, 1), 0) < lens[prompt]

    @pl.when(head == 0)
    def _():
        for r in range(rows):
            features[:, r * span : (r + 1) * span] = tok[r]
        logits = jnp.dot(features[...], wbeta[...], preferred_element_type=F32)
        rates_out[...] = jnp.where(live, jax.nn.sigmoid(logits), 0.0)

    for r in range(rows):
        weights[r * span : (r + 1) * span, :] = win[:, r].reshape(span, 3 * DK)
    total = jnp.dot(features[...], weights[...], preferred_element_type=F32)
    line[5:8, :] = prior[0].astype(F32)
    line[8:, :] = total
    mixed = taps[0:1, :] * line[5 : 5 + SEQ, :]
    for i in range(1, CONV):
        mixed += taps[i : i + 1, :] * line[5 + i : 5 + i + SEQ, :]
    active = mixed * jax.nn.sigmoid(mixed)
    query, key, value = active[:, :DK], active[:, DK : 2 * DK], active[:, 2 * DK :]
    query = query * lax.rsqrt(jnp.sum(query * query, axis=1, keepdims=True) + 1e-06)
    key = key * lax.rsqrt(jnp.sum(key * key, axis=1, keepdims=True) + 1e-06)
    key = jnp.where(live, key, 0.0).astype(BF)
    value = jnp.where(live, value, 0.0).astype(BF)
    q_out[...] = query.astype(BF)
    k_out[...] = key
    v_out[...] = value

    def copies(p, h):
        column = pl.ds(pl.multiple_of(h * DK, DK), DK)
        return [
            pltpu.make_async_copy(
                kv.at[j, pl.ds(g * PAGE, PAGE)],
                outgoing.at[spots[p * PAGES_SEQ + g], j, :, column],
                sems.at[j, g],
            )
            for j in range(2)
            for g in range(PAGES_SEQ)
        ]

    step = prompt * heads + head

    @pl.when(step > 0)
    def _():
        for copy in copies(prompt, head):
            copy.wait()

    kv[0] = key
    kv[1] = value
    for copy in copies(prompt, head):
        copy.start()

    @pl.when(step == pl.num_programs(0) * heads - 1)
    def _():
        for copy in copies(prompt, head):
            copy.wait()


def project(tokens_all, win, wbeta, taps, prior, lengths, spots, slots):
    rows, local_tokens, span = tokens_all.shape
    cols, _, depth, width = win.shape
    heads = width // (3 * DK)
    prompts = local_tokens // SEQ
    flat = jax.ShapeDtypeStruct((local_tokens, heads * DK), BF)
    block = pl.BlockSpec((SEQ, DK), lambda p, h, *_: (p, h))
    return pl.pallas_call(
        project_kernel,
        grid_spec=pltpu.PrefetchScalarGridSpec(
            num_scalar_prefetch=2,
            grid=(prompts, heads),
            in_specs=[
                pl.BlockSpec((rows, SEQ, span), lambda p, h, *_: (0, p, 0)),
                pl.BlockSpec((cols, rows, depth, 3 * DK), lambda p, h, *_: (0, 0, 0, h)),
                pl.BlockSpec((rows * span, DK), lambda p, h, *_: (0, 0)),
                pl.BlockSpec((CONV, 3 * DK), lambda p, h, *_: (0, h)),
                pl.BlockSpec((1, CONV - 1, 3 * DK), lambda p, h, *_: (p, 0, h)),
            ],
            out_specs=[
                block,
                block,
                block,
                pl.BlockSpec((SEQ, DK), lambda p, h, *_: (p, 0)),
                pl.BlockSpec(memory_space=pl.ANY),
            ],
            scratch_shapes=[
                pltpu.VMEM((SEQ + 8, 3 * DK), F32),
                pltpu.VMEM((2, SEQ, DK), BF),
                pltpu.VMEM((SEQ, rows * span), BF),
                pltpu.VMEM((rows * span, 3 * DK), BF),
                pltpu.SemaphoreType.DMA((2, PAGES_SEQ)),
            ],
        ),
        out_shape=[
            flat,
            flat,
            flat,
            jax.ShapeDtypeStruct((local_tokens, DK), F32),
            jax.ShapeDtypeStruct((slots, 2, PAGE, heads * DK), BF),
        ],
        compiler_params=pltpu.CompilerParams(vmem_limit_bytes=VMEM_LIMIT),
        cost_estimate=pl.CostEstimate(
            flops=2 * local_tokens * rows * span * width,
            bytes_accessed=30_000_000,
            transcendentals=local_tokens * width,
        ),
        name="project",
    )(lengths, spots, tokens_all, win, wbeta, taps, prior)


def mm(a, b):
    return jnp.dot(a.astype(BF), b.astype(BF), preferred_element_type=F32)


def mm_nt(a, b):
    return lax.dot_general(a, b, (((1,), (1,)), ((), ())), preferred_element_type=F32)


def mm_tn(a, b):
    return lax.dot_general(a, b, (((0,), (0,)), ((), ())), preferred_element_type=F32)


def scan_kernel(prompt, lens, picks, q_ref, k_ref, v_ref, rates, pool, gain, normed, state_out):
    heads = pool.shape[1]
    size = PAGE
    blocks = SEQ // size
    row = lax.broadcasted_iota(jnp.int32, (size, size), 0)
    column = lax.broadcasted_iota(jnp.int32, (size, size), 1)
    lower = row > column
    causal = row >= column
    eye = (row == column).astype(F32)
    items = [(c, h) for c in range(blocks) for h in range(heads)]

    def part(ref, c, h):
        return ref[c * size : (c + 1) * size, h * DK : (h + 1) * DK]

    keys = {i: part(k_ref, *i) for i in items}
    betas = {(c, h): rates[c * size : (c + 1) * size, h : h + 1] for c, h in items}
    system = {
        i: jnp.where(lower, betas[i] * mm_nt(keys[i], keys[i]), 0.0).astype(BF) for i in items
    }
    inverse = {}
    half = 1
    while half < size:
        inside = (row // (2 * half) == column // (2 * half)) & (row // half != column // half)
        for i in items:
            corner = jnp.where(inside, system[i], jnp.zeros((), BF))
            if half == 1:
                inverse[i] = eye - corner.astype(F32)
            else:
                x = inverse[i].astype(BF)
                inverse[i] = inverse[i] - mm(x, mm(corner, x))
        half *= 2
    weighted, corrections, scores = {}, {}, {}
    for i in items:
        x = inverse[i].astype(BF)
        right = jnp.concatenate(
            [(betas[i] * keys[i].astype(F32)).astype(BF), (betas[i] * part(v_ref, *i).astype(F32)).astype(BF)],
            axis=1,
        )
        solved = mm(x, right)
        weighted[i] = solved[:, :DK].astype(BF)
        corrections[i] = solved[:, DK:]
        scores[i] = jnp.where(causal, mm_nt(part(q_ref, *i), keys[i]), 0.0).astype(BF)
    states = [pool[picks[prompt, h], h] for h in range(heads)]
    for c in range(blocks):
        live = (lax.broadcasted_iota(jnp.int32, (size, 1), 0) + c * size) < lens[prompt]
        for h in range(heads):
            i = (c, h)
            both = mm(jnp.concatenate([weighted[i], part(q_ref, *i)], axis=0), states[h])
            corrected = (corrections[i] - both[:size]).astype(BF)
            out = both[size:] + mm(scores[i], corrected)
            states[h] = states[h] + mm_tn(keys[i], corrected)
            out = jnp.where(live, out, 0.0)
            scale = lax.rsqrt(jnp.mean(out * out, axis=1, keepdims=True) + 1e-05)
            normed[c * size : (c + 1) * size, h * DK : (h + 1) * DK] = (
                out * scale * gain[:, h * DK : (h + 1) * DK]
            ).astype(BF)
    for h in range(heads):
        state_out[h] = states[h]


def scan_prompt(prompt, lengths, picks, query, key, value, rates, pool, gain):
    heads = pool.shape[1]
    wide = pl.BlockSpec((SEQ, heads * DK), lambda i, *_: (prompt, 0))
    return pl.pallas_call(
        functools.partial(scan_kernel, prompt),
        grid_spec=pltpu.PrefetchScalarGridSpec(
            num_scalar_prefetch=2,
            grid=(1,),
            in_specs=[
                wide,
                wide,
                wide,
                pl.BlockSpec((SEQ, DK), lambda i, *_: (prompt, 0)),
                pl.BlockSpec(pool.shape, lambda i, *_: (0, 0, 0, 0)),
                pl.BlockSpec((1, heads * DK), lambda i, *_: (0, 0)),
            ],
            out_specs=[
                pl.BlockSpec((SEQ, heads * DK), lambda i, *_: (0, 0)),
                pl.BlockSpec((heads, DK, DK), lambda i, *_: (0, 0, 0)),
            ],
        ),
        out_shape=[
            jax.ShapeDtypeStruct((SEQ, heads * DK), BF),
            jax.ShapeDtypeStruct((heads, DK, DK), F32),
        ],
        compiler_params=pltpu.CompilerParams(vmem_limit_bytes=VMEM_LIMIT),
        cost_estimate=pl.CostEstimate(
            flops=4_000_000_000, bytes_accessed=5_000_000, transcendentals=2048
        ),
        name="scan",
    )(lengths, picks, query, key, value, rates, pool, gain)


def out_kernel(heads_all, wout, out):
    rows, _, span = heads_all.shape
    total = jnp.zeros(out.shape, F32)
    for r in range(rows):
        total += jnp.dot(heads_all[r], wout[:, r].reshape(span, out.shape[1]), preferred_element_type=F32)
    out[...] = total.astype(BF)


def out_project(heads_all, wout):
    rows, tokens, span = heads_all.shape
    width = wout.shape[3]
    return pl.pallas_call(
        out_kernel,
        out_shape=jax.ShapeDtypeStruct((tokens, width), BF),
        compiler_params=pltpu.CompilerParams(vmem_limit_bytes=VMEM_LIMIT),
        cost_estimate=pl.CostEstimate(
            flops=2 * tokens * rows * span * width, bytes_accessed=5_000_000, transcendentals=0
        ),
        name="out_project",
    )(heads_all, wout)


def col_exchange(weight):
    rows, width = weight.shape
    cols = lax.axis_size("col")
    parts = weight.reshape(rows, cols, width // cols).transpose(1, 0, 2)
    return lax.all_to_all(parts, "col", split_axis=0, concat_axis=0, tiled=True).reshape(
        rows * cols, width // cols
    )


def local(
    tokens,
    in_weight,
    out_weight,
    beta_weight,
    conv_weight,
    conv_prior,
    head_gain,
    state_pool,
    state_index,
    lengths,
    page_table,
):
    row_count = lax.axis_size("row")
    col_count = lax.axis_size("col")
    row_id = lax.axis_index("row")
    span = tokens.shape[1]
    heads = state_index.shape[1]
    prompts = lengths.shape[0]
    depth = in_weight.shape[0]

    trainer_in = in_weight.astype(BF)
    trainer_out = out_weight.astype(BF)
    in_parts = trainer_in.reshape(depth, row_count, -1).transpose(1, 0, 2)
    out_parts = trainer_out.reshape(depth, row_count, -1).transpose(1, 0, 2)
    in_rows = lax.all_to_all(in_parts, "row", split_axis=0, concat_axis=0, tiled=True)
    win = lax.all_gather(in_rows, "col", axis=0)
    tokens_all = lax.all_gather(tokens, "row", axis=0)
    out_rows = lax.all_to_all(out_parts, "row", split_axis=0, concat_axis=0, tiled=True)
    wout = lax.all_gather(out_rows, "col", axis=0)
    server_in = col_exchange(trainer_in)
    server_out = col_exchange(trainer_out)

    my_beta = lax.dynamic_slice_in_dim(beta_weight, row_id * heads, heads, 1).astype(BF)
    wbeta = jnp.pad(my_beta, ((0, 0), (0, DK - heads)))

    pages_dev = prompts * PAGES_SEQ
    capacity = max(1, 2 * pages_dev // col_count)
    slots = capacity * col_count
    targets = page_table[:, :, 0].reshape(-1)
    slot_ids = page_table[:, :, 1].reshape(-1)
    order = jnp.arange(pages_dev, dtype=jnp.int32)
    earlier = (targets[:, None] == targets[None, :]) & (order[None, :] < order[:, None])
    spots = targets * capacity + jnp.sum(earlier.astype(jnp.int32), axis=1)
    held = spots[None, :] == jnp.arange(slots, dtype=jnp.int32)[:, None]
    slot_send = jnp.sum(jnp.where(held, slot_ids[None, :] - pages_dev, 0), axis=1) + pages_dev
    arrived_slots = lax.all_to_all(slot_send, "col", split_axis=0, concat_axis=0, tiled=True)
    sources = jnp.argmax(arrived_slots[None, :] == order[:, None], axis=1).astype(jnp.int32)

    query, key, value, rates, outgoing = project(
        tokens_all, win, wbeta, conv_weight, conv_prior, lengths, spots, slots
    )
    arrived = lax.all_to_all(outgoing, "col", split_axis=0, concat_axis=0, tiled=True)

    gain = head_gain.reshape(1, -1)
    layer_parts, state_parts = [], []
    for p in range(prompts):
        normed, state = scan_prompt(p, lengths, state_index, query, key, value, rates, state_pool, gain)
        layer_parts.append(out_project(lax.all_gather(normed, "row", axis=0), wout))
        state_parts.append(state)
    layer_out = jnp.concatenate(layer_parts, axis=0)
    final_state = jnp.stack(state_parts, axis=0)
    page_cache = jnp.take(arrived, sources, axis=0, mode="clip").transpose(0, 2, 1, 3)
    return (server_in, server_out, layer_out, final_state, page_cache)


def solution(mesh):
    return jax.shard_map(
        local,
        mesh=mesh,
        in_specs=(
            P("col", "row"),
            P(("row", "col"), None),
            P(("row", "col"), None),
            P(),
            P(None, "row"),
            P("col", None, "row"),
            P("row"),
            P("col", "row", None, None),
            P("col", "row"),
            P("col"),
            P("col", None, None),
        ),
        out_specs=(
            P("row", "col"),
            P("row", "col"),
            P("col", "row"),
            P("col", "row", None, None),
            P("col", None, None, "row"),
        ),
        check_vma=False,
    )
```

```python
import functools

import jax
import jax.numpy as jnp
from jax import lax
from jax.experimental import pallas as pl
from jax.experimental.pallas import tpu as pltpu
from jax.sharding import PartitionSpec as P

DK = 128
CONV = 4
SEQ = 512
PAGE = 128
PAGES_SEQ = 4
BF = jnp.bfloat16
F32 = jnp.float32
VMEM_LIMIT = 48 * 1024 * 1024


MESH = pl.DeviceIdType.MESH


def handover_kernel(
    chain, in_parts, out_parts, tokens, win, out_rows, tokens_all, own, part_send, part_recv, tok_send, tok_recv,
    chain_send, chain_recv, pair_send, pair_recv,
):
    row, col = lax.axis_index("row"), lax.axis_index("col")
    rows = in_parts.shape[0]
    place, side = col // 2, col % 2
    twin = row + 1 - 2 * (row % 2)
    across = lax.rem(row + 2, rows)
    partner = col + 1 - 2 * side
    chunks = tok_send.shape[1]
    span = tokens.shape[0] // chunks

    barrier = pltpu.get_barrier_semaphore()
    for d in range(1, rows):
        pl.semaphore_signal(barrier, inc=1, device_id=(lax.rem(row + d, rows), col), device_id_type=MESH)
    pl.semaphore_signal(barrier, inc=1, device_id=(row, partner), device_id_type=MESH)

    @pl.when(place > 0)
    def _():
        pl.semaphore_signal(barrier, inc=1, device_id=(row, col - 2), device_id_type=MESH)

    @pl.when(place < chain - 1)
    def _():
        pl.semaphore_signal(barrier, inc=1, device_id=(row, col + 2), device_id_type=MESH)

    neighbours = lax.div(place + chain - 1, chain) + lax.div(2 * (chain - 1) - place, chain)
    pl.semaphore_wait(barrier, rows + neighbours)

    def remote(src, dst, send, recv, target):
        return pltpu.make_async_remote_copy(
            src_ref=src, dst_ref=dst, send_sem=send, recv_sem=recv, device_id=target, device_id_type=MESH
        )

    part_copies = []
    for d in range(1, rows):
        peer = lax.rem(row + d, rows)
        part_copies.append(
            remote(in_parts.at[peer], win.at[col, row], part_send.at[0, d], part_recv.at[0, d], (peer, col))
        )
        part_copies.append(
            remote(out_parts.at[peer], out_rows.at[row], part_send.at[1, d], part_recv.at[1, d], (peer, col))
        )
    for copy in part_copies:
        copy.start()
    own_copies = [
        pltpu.make_async_copy(in_parts.at[row], win.at[col, row], own.at[0]),
        pltpu.make_async_copy(out_parts.at[row], out_rows.at[row], own.at[1]),
        pltpu.make_async_copy(tokens, tokens_all.at[row], own.at[2]),
    ]
    for copy in own_copies:
        copy.start()

    def chunk(slot, n):
        return tokens_all.at[slot, pl.ds(n * span, span)]

    def token_copy(kind, n):
        mine = tokens.at[pl.ds(n * span, span)]
        src = chunk(across, n) if kind == 2 else mine
        dst = chunk(across if kind == 2 else row, n)
        target = (across, col) if kind == 0 else (twin, col)
        return remote(src, dst, tok_send.at[kind, n], tok_recv.at[kind, n], target)

    for n in range(chunks):
        token_copy(0, n).start()
    for n in range(chunks):
        token_copy(1, n).start()

    def chain_copy(way, s):
        block = col - 2 * s if way == 0 else col + 2 * s
        target = (row, col + 2) if way == 0 else (row, col - 2)
        return remote(
            win.at[block], win.at[block], chain_send.at[way, s], chain_recv.at[way, s], target
        )

    def pair_copy(way, s):
        block = col - 2 * s if way == 0 else col + 2 * s
        return remote(win.at[block], win.at[block], pair_send.at[way, s], pair_recv.at[way, s], (row, partner))

    def held(way, s):
        return place - s >= 0 if way == 0 else place + s < chain

    def goes_on(way):
        return place < chain - 1 if way == 0 else place > 0

    own_copies[0].wait()
    for d in range(1, rows):
        part_copies[2 * (d - 1)].wait_recv()
    for s in range(chain):
        for way in range(2):

            @pl.when(held(way, s))
            def _():
                if s > 0:
                    chain_copy(way, s - 1).wait_recv()

                @pl.when(goes_on(way))
                def _():
                    chain_copy(way, s).start()

                if s > 0 or way == 0:
                    pair_copy(way, s).start()

        if 0 < s <= chunks:
            token_copy(0, s - 1).wait_recv()
            token_copy(2, s - 1).start()
    for n in range(max(0, chain - 1), chunks):
        token_copy(0, n).wait_recv()
        token_copy(2, n).start()
    for n in range(chunks):
        token_copy(1, n).wait_recv()
        token_copy(2, n).wait_recv()
        for kind in range(3):
            token_copy(kind, n).wait_send()
    for d in range(1, rows):
        part_copies[2 * (d - 1)].wait_send()
        part_copies[2 * (d - 1) + 1].wait()
    own_copies[1].wait()
    own_copies[2].wait()
    for s in range(chain):
        for way in range(2):

            @pl.when(held(way, s))
            def _():
                @pl.when(goes_on(way))
                def _():
                    chain_copy(way, s).wait_send()

                if s > 0 or way == 0:
                    pair_copy(way, s).wait()


def handover(in_parts, out_parts, tokens, cols):
    rows, depth, width = in_parts.shape
    chain = cols // 2
    chunks = tokens.shape[0] // SEQ
    dma = pltpu.SemaphoreType.DMA
    anywhere = pl.BlockSpec(memory_space=pl.ANY)
    return pl.pallas_call(
        functools.partial(handover_kernel, chain),
        in_specs=[anywhere] * 3,
        out_specs=[anywhere] * 3,
        out_shape=[
            jax.ShapeDtypeStruct((cols, rows, depth, width), BF),
            jax.ShapeDtypeStruct(out_parts.shape, BF),
            jax.ShapeDtypeStruct((rows,) + tokens.shape, BF),
        ],
        scratch_shapes=[
            dma((3,)),
            dma((2, rows)),
            dma((2, rows)),
            dma((3, chunks)),
            dma((3, chunks)),
            dma((2, chain)),
            dma((2, chain)),
            dma((2, chain)),
            dma((2, chain)),
        ],
        compiler_params=pltpu.CompilerParams(
            collective_id=0, has_side_effects=True, vmem_limit_bytes=VMEM_LIMIT
        ),
        cost_estimate=pl.CostEstimate(flops=0, bytes_accessed=300_000_000, transcendentals=0),
        name="handover",
    )(in_parts, out_parts, tokens)


def project_kernel(
    lens, spots, tok, win, wbeta, taps, prior, q_out, k_out, v_out, rates_out, outgoing, line, kv, features, weights, sems
):
    prompt, head = pl.program_id(0), pl.program_id(1)
    heads = pl.num_programs(1)
    rows = tok.shape[0]
    span = tok.shape[2]
    live = lax.broadcasted_iota(jnp.int32, (SEQ, 1), 0) < lens[prompt]

    @pl.when(head == 0)
    def _():
        for r in range(rows):
            features[:, r * span : (r + 1) * span] = tok[r]
        logits = jnp.dot(features[...], wbeta[...], preferred_element_type=F32)
        rates_out[...] = jnp.where(live, jax.nn.sigmoid(logits), 0.0)

    for r in range(rows):
        weights[r * span : (r + 1) * span, :] = win[:, r].reshape(span, 3 * DK)
    total = jnp.dot(features[...], weights[...], preferred_element_type=F32)
    line[5:8, :] = prior[0].astype(F32)
    line[8:, :] = total
    mixed = taps[0:1, :] * line[5 : 5 + SEQ, :]
    for i in range(1, CONV):
        mixed += taps[i : i + 1, :] * line[5 + i : 5 + i + SEQ, :]
    active = mixed * jax.nn.sigmoid(mixed)
    query, key, value = active[:, :DK], active[:, DK : 2 * DK], active[:, 2 * DK :]
    query = query * lax.rsqrt(jnp.sum(query * query, axis=1, keepdims=True) + 1e-06)
    key = key * lax.rsqrt(jnp.sum(key * key, axis=1, keepdims=True) + 1e-06)
    key = jnp.where(live, key, 0.0).astype(BF)
    value = jnp.where(live, value, 0.0).astype(BF)
    q_out[...] = query.astype(BF)
    k_out[...] = key
    v_out[...] = value

    def copies(p, h):
        column = pl.ds(pl.multiple_of(h * DK, DK), DK)
        return [
            pltpu.make_async_copy(
                kv.at[j, pl.ds(g * PAGE, PAGE)],
                outgoing.at[spots[p * PAGES_SEQ + g], j, :, column],
                sems.at[j, g],
            )
            for j in range(2)
            for g in range(PAGES_SEQ)
        ]

    step = prompt * heads + head

    @pl.when(step > 0)
    def _():
        for copy in copies(prompt, head):
            copy.wait()

    kv[0] = key
    kv[1] = value
    for copy in copies(prompt, head):
        copy.start()

    @pl.when(step == pl.num_programs(0) * heads - 1)
    def _():
        for copy in copies(prompt, head):
            copy.wait()


def project(tokens_all, win, wbeta, taps, prior, lengths, spots, slots):
    rows, local_tokens, span = tokens_all.shape
    cols, _, depth, width = win.shape
    heads = width // (3 * DK)
    prompts = local_tokens // SEQ
    flat = jax.ShapeDtypeStruct((local_tokens, heads * DK), BF)
    block = pl.BlockSpec((SEQ, DK), lambda p, h, *_: (p, h))
    return pl.pallas_call(
        project_kernel,
        grid_spec=pltpu.PrefetchScalarGridSpec(
            num_scalar_prefetch=2,
            grid=(prompts, heads),
            in_specs=[
                pl.BlockSpec((rows, SEQ, span), lambda p, h, *_: (0, p, 0)),
                pl.BlockSpec((cols, rows, depth, 3 * DK), lambda p, h, *_: (0, 0, 0, h)),
                pl.BlockSpec((rows * span, DK), lambda p, h, *_: (0, 0)),
                pl.BlockSpec((CONV, 3 * DK), lambda p, h, *_: (0, h)),
                pl.BlockSpec((1, CONV - 1, 3 * DK), lambda p, h, *_: (p, 0, h)),
            ],
            out_specs=[
                block,
                block,
                block,
                pl.BlockSpec((SEQ, DK), lambda p, h, *_: (p, 0)),
                pl.BlockSpec(memory_space=pl.ANY),
            ],
            scratch_shapes=[
                pltpu.VMEM((SEQ + 8, 3 * DK), F32),
                pltpu.VMEM((2, SEQ, DK), BF),
                pltpu.VMEM((SEQ, rows * span), BF),
                pltpu.VMEM((rows * span, 3 * DK), BF),
                pltpu.SemaphoreType.DMA((2, PAGES_SEQ)),
            ],
        ),
        out_shape=[
            flat,
            flat,
            flat,
            jax.ShapeDtypeStruct((local_tokens, DK), F32),
            jax.ShapeDtypeStruct((slots, 2, PAGE, heads * DK), BF),
        ],
        compiler_params=pltpu.CompilerParams(vmem_limit_bytes=VMEM_LIMIT),
        cost_estimate=pl.CostEstimate(
            flops=2 * local_tokens * rows * span * width,
            bytes_accessed=30_000_000,
            transcendentals=local_tokens * width,
        ),
        name="project",
    )(lengths, spots, tokens_all, win, wbeta, taps, prior)


def mm(a, b):
    return jnp.dot(a.astype(BF), b.astype(BF), preferred_element_type=F32)


def mm_nt(a, b):
    return lax.dot_general(a, b, (((1,), (1,)), ((), ())), preferred_element_type=F32)


def mm_tn(a, b):
    return lax.dot_general(a, b, (((0,), (0,)), ((), ())), preferred_element_type=F32)


def scan_kernel(prompt, lens, picks, q_ref, k_ref, v_ref, rates, pool, gain, normed, state_out):
    heads = pool.shape[1]
    size = PAGE
    blocks = SEQ // size
    row = lax.broadcasted_iota(jnp.int32, (size, size), 0)
    column = lax.broadcasted_iota(jnp.int32, (size, size), 1)
    lower = row > column
    causal = row >= column
    eye = (row == column).astype(F32)
    items = [(c, h) for c in range(blocks) for h in range(heads)]

    def part(ref, c, h):
        return ref[c * size : (c + 1) * size, h * DK : (h + 1) * DK]

    keys = {i: part(k_ref, *i) for i in items}
    betas = {(c, h): rates[c * size : (c + 1) * size, h : h + 1] for c, h in items}
    system = {
        i: jnp.where(lower, betas[i] * mm_nt(keys[i], keys[i]), 0.0).astype(BF) for i in items
    }
    inverse = {}
    half = 1
    while half < size:
        inside = (row // (2 * half) == column // (2 * half)) & (row // half != column // half)
        for i in items:
            corner = jnp.where(inside, system[i], jnp.zeros((), BF))
            if half == 1:
                inverse[i] = eye - corner.astype(F32)
            else:
                x = inverse[i].astype(BF)
                inverse[i] = inverse[i] - mm(x, mm(corner, x))
        half *= 2
    weighted, corrections, scores = {}, {}, {}
    for i in items:
        x = inverse[i].astype(BF)
        right = jnp.concatenate(
            [(betas[i] * keys[i].astype(F32)).astype(BF), (betas[i] * part(v_ref, *i).astype(F32)).astype(BF)],
            axis=1,
        )
        solved = mm(x, right)
        weighted[i] = solved[:, :DK].astype(BF)
        corrections[i] = solved[:, DK:]
        scores[i] = jnp.where(causal, mm_nt(part(q_ref, *i), keys[i]), 0.0).astype(BF)
    states = [pool[picks[prompt, h], h] for h in range(heads)]
    for c in range(blocks):
        live = (lax.broadcasted_iota(jnp.int32, (size, 1), 0) + c * size) < lens[prompt]
        for h in range(heads):
            i = (c, h)
            both = mm(jnp.concatenate([weighted[i], part(q_ref, *i)], axis=0), states[h])
            corrected = (corrections[i] - both[:size]).astype(BF)
            out = both[size:] + mm(scores[i], corrected)
            states[h] = states[h] + mm_tn(keys[i], corrected)
            out = jnp.where(live, out, 0.0)
            scale = lax.rsqrt(jnp.mean(out * out, axis=1, keepdims=True) + 1e-05)
            normed[c * size : (c + 1) * size, h * DK : (h + 1) * DK] = (
                out * scale * gain[:, h * DK : (h + 1) * DK]
            ).astype(BF)
    for h in range(heads):
        state_out[h] = states[h]


def scan_prompt(prompt, lengths, picks, query, key, value, rates, pool, gain):
    heads = pool.shape[1]
    wide = pl.BlockSpec((SEQ, heads * DK), lambda i, *_: (prompt, 0))
    return pl.pallas_call(
        functools.partial(scan_kernel, prompt),
        grid_spec=pltpu.PrefetchScalarGridSpec(
            num_scalar_prefetch=2,
            grid=(1,),
            in_specs=[
                wide,
                wide,
                wide,
                pl.BlockSpec((SEQ, DK), lambda i, *_: (prompt, 0)),
                pl.BlockSpec(pool.shape, lambda i, *_: (0, 0, 0, 0)),
                pl.BlockSpec((1, heads * DK), lambda i, *_: (0, 0)),
            ],
            out_specs=[
                pl.BlockSpec((SEQ, heads * DK), lambda i, *_: (0, 0)),
                pl.BlockSpec((heads, DK, DK), lambda i, *_: (0, 0, 0)),
            ],
        ),
        out_shape=[
            jax.ShapeDtypeStruct((SEQ, heads * DK), BF),
            jax.ShapeDtypeStruct((heads, DK, DK), F32),
        ],
        compiler_params=pltpu.CompilerParams(vmem_limit_bytes=VMEM_LIMIT),
        cost_estimate=pl.CostEstimate(
            flops=4_000_000_000, bytes_accessed=5_000_000, transcendentals=2048
        ),
        name="scan",
    )(lengths, picks, query, key, value, rates, pool, gain)


def out_kernel(heads_all, wout, out):
    rows, _, span = heads_all.shape
    total = jnp.zeros(out.shape, F32)
    for r in range(rows):
        total += jnp.dot(heads_all[r], wout[:, r].reshape(span, out.shape[1]), preferred_element_type=F32)
    out[...] = total.astype(BF)


def out_project(heads_all, wout):
    rows, tokens, span = heads_all.shape
    width = wout.shape[3]
    return pl.pallas_call(
        out_kernel,
        out_shape=jax.ShapeDtypeStruct((tokens, width), BF),
        compiler_params=pltpu.CompilerParams(vmem_limit_bytes=VMEM_LIMIT),
        cost_estimate=pl.CostEstimate(
            flops=2 * tokens * rows * span * width, bytes_accessed=5_000_000, transcendentals=0
        ),
        name="out_project",
    )(heads_all, wout)


def col_exchange(weight):
    rows, width = weight.shape
    cols = lax.axis_size("col")
    parts = weight.reshape(rows, cols, width // cols).transpose(1, 0, 2)
    return lax.all_to_all(parts, "col", split_axis=0, concat_axis=0, tiled=True).reshape(
        rows * cols, width // cols
    )


def local(
    tokens,
    in_weight,
    out_weight,
    beta_weight,
    conv_weight,
    conv_prior,
    head_gain,
    state_pool,
    state_index,
    lengths,
    page_table,
):
    row_count = lax.axis_size("row")
    col_count = lax.axis_size("col")
    row_id = lax.axis_index("row")
    span = tokens.shape[1]
    heads = state_index.shape[1]
    prompts = lengths.shape[0]
    depth = in_weight.shape[0]

    trainer_in = in_weight.astype(BF)
    trainer_out = out_weight.astype(BF)
    in_parts = trainer_in.reshape(depth, row_count, -1).transpose(1, 0, 2)
    out_parts = trainer_out.reshape(depth, row_count, -1).transpose(1, 0, 2)
    win, out_rows, tokens_all = handover(in_parts, out_parts, tokens, col_count)
    wout = lax.all_gather(out_rows, "col", axis=0)

    my_beta = lax.dynamic_slice_in_dim(beta_weight, row_id * heads, heads, 1).astype(BF)
    wbeta = jnp.pad(my_beta, ((0, 0), (0, DK - heads)))

    pages_dev = prompts * PAGES_SEQ
    capacity = max(1, 2 * pages_dev // col_count)
    slots = capacity * col_count
    targets = page_table[:, :, 0].reshape(-1)
    slot_ids = page_table[:, :, 1].reshape(-1)
    order = jnp.arange(pages_dev, dtype=jnp.int32)
    earlier = (targets[:, None] == targets[None, :]) & (order[None, :] < order[:, None])
    spots = targets * capacity + jnp.sum(earlier.astype(jnp.int32), axis=1)
    held = spots[None, :] == jnp.arange(slots, dtype=jnp.int32)[:, None]
    slot_send = jnp.sum(jnp.where(held, slot_ids[None, :] - pages_dev, 0), axis=1) + pages_dev
    arrived_slots = lax.all_to_all(slot_send, "col", split_axis=0, concat_axis=0, tiled=True)
    sources = jnp.argmax(arrived_slots[None, :] == order[:, None], axis=1).astype(jnp.int32)

    query, key, value, rates, outgoing = project(
        tokens_all, win, wbeta, conv_weight, conv_prior, lengths, spots, slots
    )
    trainer_in, trainer_out, rates = lax.optimization_barrier((trainer_in, trainer_out, rates))
    server_in = col_exchange(trainer_in)
    server_out = col_exchange(trainer_out)
    arrived = lax.all_to_all(outgoing, "col", split_axis=0, concat_axis=0, tiled=True)

    gain = head_gain.reshape(1, -1)
    layer_parts, state_parts = [], []
    for p in range(prompts):
        normed, state = scan_prompt(p, lengths, state_index, query, key, value, rates, state_pool, gain)
        layer_parts.append(out_project(lax.all_gather(normed, "row", axis=0), wout))
        state_parts.append(state)
    layer_out = jnp.concatenate(layer_parts, axis=0)
    final_state = jnp.stack(state_parts, axis=0)
    page_cache = jnp.take(arrived, sources, axis=0, mode="clip").transpose(0, 2, 1, 3)
    return (server_in, server_out, layer_out, final_state, page_cache)


def solution(mesh):
    return jax.shard_map(
        local,
        mesh=mesh,
        in_specs=(
            P("col", "row"),
            P(("row", "col"), None),
            P(("row", "col"), None),
            P(),
            P(None, "row"),
            P("col", None, "row"),
            P("row"),
            P("col", "row", None, None),
            P("col", "row"),
            P("col"),
            P("col", None, None),
        ),
        out_specs=(
            P("row", "col"),
            P("row", "col"),
            P("col", "row"),
            P("col", "row", None, None),
            P("col", None, None, "row"),
        ),
        check_vma=False,
    )
```

```python
import functools

import jax
import jax.numpy as jnp
from jax import lax
from jax.experimental import pallas as pl
from jax.experimental.pallas import tpu as pltpu
from jax.sharding import PartitionSpec as P

DK = 128
CONV = 4
SEQ = 512
PAGE = 128
PAGES_SEQ = 4
BF = jnp.bfloat16
F32 = jnp.float32
VMEM_LIMIT = 48 * 1024 * 1024


MESH = pl.DeviceIdType.MESH


def handover_kernel(
    chain, in_parts, out_parts, in_blocks, out_blocks, tokens, win, out_rows, server_in, server_out, tokens_all, own, part_send, part_recv, tok_send, tok_recv,
    chain_send, chain_recv, pair_send, pair_recv, block_send, block_recv,
):
    row, col = lax.axis_index("row"), lax.axis_index("col")
    rows, cols = in_parts.shape[0], in_blocks.shape[0]
    place, side = col // 2, col % 2
    twin = row + 1 - 2 * (row % 2)
    across = lax.rem(row + 2, rows)
    partner = col + 1 - 2 * side
    chunks = tok_send.shape[1]
    span = tokens.shape[0] // chunks

    barrier = pltpu.get_barrier_semaphore()
    for d in range(1, rows):
        pl.semaphore_signal(barrier, inc=1, device_id=(lax.rem(row + d, rows), col), device_id_type=MESH)
    for d in range(1, cols):
        pl.semaphore_signal(barrier, inc=1, device_id=(row, lax.rem(col + d, cols)), device_id_type=MESH)
    pl.semaphore_wait(barrier, rows - 1 + cols - 1)

    def remote(src, dst, send, recv, target):
        return pltpu.make_async_remote_copy(
            src_ref=src, dst_ref=dst, send_sem=send, recv_sem=recv, device_id=target, device_id_type=MESH
        )

    part_copies = []
    for d in range(1, rows):
        peer = lax.rem(row + d, rows)
        part_copies.append(
            remote(in_parts.at[peer], win.at[col, row], part_send.at[0, d], part_recv.at[0, d], (peer, col))
        )
        part_copies.append(
            remote(out_parts.at[peer], out_rows.at[row], part_send.at[1, d], part_recv.at[1, d], (peer, col))
        )
    for copy in part_copies:
        copy.start()
    own_copies = [
        pltpu.make_async_copy(in_parts.at[row], win.at[col, row], own.at[0]),
        pltpu.make_async_copy(out_parts.at[row], out_rows.at[row], own.at[1]),
        pltpu.make_async_copy(tokens, tokens_all.at[row], own.at[2]),
        pltpu.make_async_copy(in_blocks.at[col], server_in.at[col], own.at[3]),
        pltpu.make_async_copy(out_blocks.at[col], server_out.at[col], own.at[4]),
    ]
    for copy in own_copies:
        copy.start()

    def chunk(slot, n):
        return tokens_all.at[slot, pl.ds(n * span, span)]

    def token_copy(kind, n):
        mine = tokens.at[pl.ds(n * span, span)]
        src = chunk(across, n) if kind == 2 else mine
        dst = chunk(across if kind == 2 else row, n)
        target = (across, col) if kind == 0 else (twin, col)
        return remote(src, dst, tok_send.at[kind, n], tok_recv.at[kind, n], target)

    for n in range(chunks):
        token_copy(0, n).start()
    for n in range(chunks):
        token_copy(1, n).start()

    def chain_copy(way, s):
        block = col - 2 * s if way == 0 else col + 2 * s
        target = (row, col + 2) if way == 0 else (row, col - 2)
        return remote(
            win.at[block], win.at[block], chain_send.at[way, s], chain_recv.at[way, s], target
        )

    def pair_copy(way, s):
        block = col - 2 * s if way == 0 else col + 2 * s
        return remote(win.at[block], win.at[block], pair_send.at[way, s], pair_recv.at[way, s], (row, partner))

    def held(way, s):
        return place - s >= 0 if way == 0 else place + s < chain

    def goes_on(way):
        return place < chain - 1 if way == 0 else place > 0

    own_copies[0].wait()
    for d in range(1, rows):
        part_copies[2 * (d - 1)].wait_recv()
    for s in range(chain):
        for way in range(2):

            @pl.when(held(way, s))
            def _():
                if s > 0:
                    chain_copy(way, s - 1).wait_recv()

                @pl.when(goes_on(way))
                def _():
                    chain_copy(way, s).start()

                if s > 0 or way == 0:
                    pair_copy(way, s).start()

        if 0 < s <= chunks:
            token_copy(0, s - 1).wait_recv()
            token_copy(2, s - 1).start()
    block_copies = []
    for d in range(1, cols):
        peer = lax.rem(col + d, cols)
        block_copies.append(
            remote(in_blocks.at[peer], server_in.at[col], block_send.at[0, d], block_recv.at[0, d], (row, peer))
        )
        block_copies.append(
            remote(out_blocks.at[peer], server_out.at[col], block_send.at[1, d], block_recv.at[1, d], (row, peer))
        )
    for copy in block_copies:
        copy.start()
    for n in range(max(0, chain - 1), chunks):
        token_copy(0, n).wait_recv()
        token_copy(2, n).start()
    for n in range(chunks):
        token_copy(1, n).wait_recv()
        token_copy(2, n).wait_recv()
        for kind in range(3):
            token_copy(kind, n).wait_send()
    for d in range(1, rows):
        part_copies[2 * (d - 1)].wait_send()
        part_copies[2 * (d - 1) + 1].wait()
    for copy in own_copies[1:]:
        copy.wait()
    for s in range(chain):
        for way in range(2):

            @pl.when(held(way, s))
            def _():
                @pl.when(goes_on(way))
                def _():
                    chain_copy(way, s).wait_send()

                if s > 0 or way == 0:
                    pair_copy(way, s).wait()

    for copy in block_copies:
        copy.wait()


def handover(in_parts, out_parts, in_blocks, out_blocks, tokens, cols):
    rows, depth, width = in_parts.shape
    chain = cols // 2
    chunks = tokens.shape[0] // SEQ
    dma = pltpu.SemaphoreType.DMA
    anywhere = pl.BlockSpec(memory_space=pl.ANY)
    return pl.pallas_call(
        functools.partial(handover_kernel, chain),
        in_specs=[anywhere] * 5,
        out_specs=[anywhere] * 5,
        out_shape=[
            jax.ShapeDtypeStruct((cols, rows, depth, width), BF),
            jax.ShapeDtypeStruct(out_parts.shape, BF),
            jax.ShapeDtypeStruct(in_blocks.shape, BF),
            jax.ShapeDtypeStruct(out_blocks.shape, BF),
            jax.ShapeDtypeStruct((rows,) + tokens.shape, BF),
        ],
        scratch_shapes=[
            dma((5,)),
            dma((2, rows)),
            dma((2, rows)),
            dma((3, chunks)),
            dma((3, chunks)),
            dma((2, chain)),
            dma((2, chain)),
            dma((2, chain)),
            dma((2, chain)),
            dma((2, cols)),
            dma((2, cols)),
        ],
        compiler_params=pltpu.CompilerParams(
            collective_id=0, has_side_effects=True, vmem_limit_bytes=VMEM_LIMIT
        ),
        cost_estimate=pl.CostEstimate(flops=0, bytes_accessed=300_000_000, transcendentals=0),
        name="handover",
    )(in_parts, out_parts, in_blocks, out_blocks, tokens)


def row_gather_kernel(mine, whole, own, send, recv):
    row, col = lax.axis_index("row"), lax.axis_index("col")
    rows = whole.shape[0]
    twin = row + 1 - 2 * (row % 2)
    across = lax.rem(row + 2, rows)
    chunks = send.shape[1]
    span = mine.shape[0] // chunks

    barrier = pltpu.get_barrier_semaphore()
    for peer in (twin, across):
        pl.semaphore_signal(barrier, inc=1, device_id=(peer, col), device_id_type=MESH)
    pl.semaphore_wait(barrier, 2)

    def copy(kind, n):
        piece = pl.ds(n * span, span)
        slot = across if kind == 2 else row
        return pltpu.make_async_remote_copy(
            src_ref=whole.at[across, piece] if kind == 2 else mine.at[piece],
            dst_ref=whole.at[slot, piece],
            send_sem=send.at[kind, n],
            recv_sem=recv.at[kind, n],
            device_id=(across if kind == 0 else twin, col),
            device_id_type=MESH,
        )

    local_copy = pltpu.make_async_copy(mine, whole.at[row], own)
    for kind in range(2):
        for n in range(chunks):
            copy(kind, n).start()
    local_copy.start()
    for n in range(chunks):
        copy(0, n).wait_recv()
        copy(2, n).start()
    for n in range(chunks):
        copy(0, n).wait_send()
        copy(1, n).wait()
        copy(2, n).wait()
    local_copy.wait()


def row_gather(mine, rows):
    chunks = mine.shape[0] // SEQ
    dma = pltpu.SemaphoreType.DMA
    return pl.pallas_call(
        row_gather_kernel,
        in_specs=[pl.BlockSpec(memory_space=pl.ANY)],
        out_specs=pl.BlockSpec(memory_space=pl.ANY),
        out_shape=jax.ShapeDtypeStruct((rows,) + mine.shape, BF),
        scratch_shapes=[dma(()), dma((3, chunks)), dma((3, chunks))],
        compiler_params=pltpu.CompilerParams(
            collective_id=1, has_side_effects=True, vmem_limit_bytes=VMEM_LIMIT
        ),
        cost_estimate=pl.CostEstimate(flops=0, bytes_accessed=100_000_000, transcendentals=0),
        name="row_gather",
    )(mine)


def project_kernel(
    lens, spots, tok, win, wbeta, taps, prior, q_out, k_out, v_out, rates_out, outgoing, line, kv, features, weights, sems
):
    prompt, head = pl.program_id(0), pl.program_id(1)
    heads = pl.num_programs(1)
    rows = tok.shape[0]
    span = tok.shape[2]
    live = lax.broadcasted_iota(jnp.int32, (SEQ, 1), 0) < lens[prompt]

    @pl.when(head == 0)
    def _():
        for r in range(rows):
            features[:, r * span : (r + 1) * span] = tok[r]
        logits = jnp.dot(features[...], wbeta[...], preferred_element_type=F32)
        rates_out[...] = jnp.where(live, jax.nn.sigmoid(logits), 0.0)

    for r in range(rows):
        weights[r * span : (r + 1) * span, :] = win[:, r].reshape(span, 3 * DK)
    total = jnp.dot(features[...], weights[...], preferred_element_type=F32)
    line[5:8, :] = prior[0].astype(F32)
    line[8:, :] = total
    mixed = taps[0:1, :] * line[5 : 5 + SEQ, :]
    for i in range(1, CONV):
        mixed += taps[i : i + 1, :] * line[5 + i : 5 + i + SEQ, :]
    active = mixed * jax.nn.sigmoid(mixed)
    query, key, value = active[:, :DK], active[:, DK : 2 * DK], active[:, 2 * DK :]
    query = query * lax.rsqrt(jnp.sum(query * query, axis=1, keepdims=True) + 1e-06)
    key = key * lax.rsqrt(jnp.sum(key * key, axis=1, keepdims=True) + 1e-06)
    key = jnp.where(live, key, 0.0).astype(BF)
    value = jnp.where(live, value, 0.0).astype(BF)
    q_out[...] = query.astype(BF)
    k_out[...] = key
    v_out[...] = value

    def copies(p, h):
        column = pl.ds(pl.multiple_of(h * DK, DK), DK)
        return [
            pltpu.make_async_copy(
                kv.at[j, pl.ds(g * PAGE, PAGE)],
                outgoing.at[spots[p * PAGES_SEQ + g], j, :, column],
                sems.at[j, g],
            )
            for j in range(2)
            for g in range(PAGES_SEQ)
        ]

    step = prompt * heads + head

    @pl.when(step > 0)
    def _():
        for copy in copies(prompt, head):
            copy.wait()

    kv[0] = key
    kv[1] = value
    for copy in copies(prompt, head):
        copy.start()

    @pl.when(step == pl.num_programs(0) * heads - 1)
    def _():
        for copy in copies(prompt, head):
            copy.wait()


def project(tokens_all, win, wbeta, taps, prior, lengths, spots, slots):
    rows, local_tokens, span = tokens_all.shape
    cols, _, depth, width = win.shape
    heads = width // (3 * DK)
    prompts = local_tokens // SEQ
    flat = jax.ShapeDtypeStruct((local_tokens, heads * DK), BF)
    block = pl.BlockSpec((SEQ, DK), lambda p, h, *_: (p, h))
    return pl.pallas_call(
        project_kernel,
        grid_spec=pltpu.PrefetchScalarGridSpec(
            num_scalar_prefetch=2,
            grid=(prompts, heads),
            in_specs=[
                pl.BlockSpec((rows, SEQ, span), lambda p, h, *_: (0, p, 0)),
                pl.BlockSpec((cols, rows, depth, 3 * DK), lambda p, h, *_: (0, 0, 0, h)),
                pl.BlockSpec((rows * span, DK), lambda p, h, *_: (0, 0)),
                pl.BlockSpec((CONV, 3 * DK), lambda p, h, *_: (0, h)),
                pl.BlockSpec((1, CONV - 1, 3 * DK), lambda p, h, *_: (p, 0, h)),
            ],
            out_specs=[
                block,
                block,
                block,
                pl.BlockSpec((SEQ, DK), lambda p, h, *_: (p, 0)),
                pl.BlockSpec(memory_space=pl.ANY),
            ],
            scratch_shapes=[
                pltpu.VMEM((SEQ + 8, 3 * DK), F32),
                pltpu.VMEM((2, SEQ, DK), BF),
                pltpu.VMEM((SEQ, rows * span), BF),
                pltpu.VMEM((rows * span, 3 * DK), BF),
                pltpu.SemaphoreType.DMA((2, PAGES_SEQ)),
            ],
        ),
        out_shape=[
            flat,
            flat,
            flat,
            jax.ShapeDtypeStruct((local_tokens, DK), F32),
            jax.ShapeDtypeStruct((slots, 2, PAGE, heads * DK), BF),
        ],
        compiler_params=pltpu.CompilerParams(vmem_limit_bytes=VMEM_LIMIT),
        cost_estimate=pl.CostEstimate(
            flops=2 * local_tokens * rows * span * width,
            bytes_accessed=30_000_000,
            transcendentals=local_tokens * width,
        ),
        name="project",
    )(lengths, spots, tokens_all, win, wbeta, taps, prior)


def mm(a, b):
    return jnp.dot(a.astype(BF), b.astype(BF), preferred_element_type=F32)


def mm_nt(a, b):
    return lax.dot_general(a, b, (((1,), (1,)), ((), ())), preferred_element_type=F32)


def mm_tn(a, b):
    return lax.dot_general(a, b, (((0,), (0,)), ((), ())), preferred_element_type=F32)


def scan_kernel(lens, picks, q_ref, k_ref, v_ref, rates, pool, gain, normed, state_out):
    prompt = pl.program_id(0)
    heads = pool.shape[1]
    size = PAGE
    blocks = SEQ // size
    row = lax.broadcasted_iota(jnp.int32, (size, size), 0)
    column = lax.broadcasted_iota(jnp.int32, (size, size), 1)
    lower = row > column
    causal = row >= column
    eye = (row == column).astype(F32)
    items = [(c, h) for c in range(blocks) for h in range(heads)]

    def part(ref, c, h):
        return ref[c * size : (c + 1) * size, h * DK : (h + 1) * DK]

    keys = {i: part(k_ref, *i) for i in items}
    betas = {(c, h): rates[c * size : (c + 1) * size, h : h + 1] for c, h in items}
    system = {
        i: jnp.where(lower, betas[i] * mm_nt(keys[i], keys[i]), 0.0).astype(BF) for i in items
    }
    inverse = {}
    half = 1
    while half < size:
        inside = (row // (2 * half) == column // (2 * half)) & (row // half != column // half)
        for i in items:
            corner = jnp.where(inside, system[i], jnp.zeros((), BF))
            if half == 1:
                inverse[i] = eye - corner.astype(F32)
            else:
                x = inverse[i].astype(BF)
                inverse[i] = inverse[i] - mm(x, mm(corner, x))
        half *= 2
    weighted, corrections, scores = {}, {}, {}
    for i in items:
        x = inverse[i].astype(BF)
        right = jnp.concatenate(
            [(betas[i] * keys[i].astype(F32)).astype(BF), (betas[i] * part(v_ref, *i).astype(F32)).astype(BF)],
            axis=1,
        )
        solved = mm(x, right)
        weighted[i] = solved[:, :DK].astype(BF)
        corrections[i] = solved[:, DK:]
        scores[i] = jnp.where(causal, mm_nt(part(q_ref, *i), keys[i]), 0.0).astype(BF)
    states = [pool[picks[prompt, h], h] for h in range(heads)]
    for c in range(blocks):
        live = (lax.broadcasted_iota(jnp.int32, (size, 1), 0) + c * size) < lens[prompt]
        for h in range(heads):
            i = (c, h)
            both = mm(jnp.concatenate([weighted[i], part(q_ref, *i)], axis=0), states[h])
            corrected = (corrections[i] - both[:size]).astype(BF)
            out = both[size:] + mm(scores[i], corrected)
            states[h] = states[h] + mm_tn(keys[i], corrected)
            out = jnp.where(live, out, 0.0)
            scale = lax.rsqrt(jnp.mean(out * out, axis=1, keepdims=True) + 1e-05)
            normed[c * size : (c + 1) * size, h * DK : (h + 1) * DK] = (
                out * scale * gain[:, h * DK : (h + 1) * DK]
            ).astype(BF)
    for h in range(heads):
        state_out[0, h] = states[h]


def scan_all(lengths, picks, query, key, value, rates, pool, gain):
    heads = pool.shape[1]
    prompts = query.shape[0] // SEQ
    wide = pl.BlockSpec((SEQ, heads * DK), lambda i, *_: (i, 0))
    return pl.pallas_call(
        scan_kernel,
        grid_spec=pltpu.PrefetchScalarGridSpec(
            num_scalar_prefetch=2,
            grid=(prompts,),
            in_specs=[
                wide,
                wide,
                wide,
                pl.BlockSpec((SEQ, DK), lambda i, *_: (i, 0)),
                pl.BlockSpec(pool.shape, lambda i, *_: (0, 0, 0, 0)),
                pl.BlockSpec((1, heads * DK), lambda i, *_: (0, 0)),
            ],
            out_specs=[
                wide,
                pl.BlockSpec((1, heads, DK, DK), lambda i, *_: (i, 0, 0, 0)),
            ],
        ),
        out_shape=[
            jax.ShapeDtypeStruct(query.shape, BF),
            jax.ShapeDtypeStruct((prompts, heads, DK, DK), F32),
        ],
        compiler_params=pltpu.CompilerParams(vmem_limit_bytes=VMEM_LIMIT),
        cost_estimate=pl.CostEstimate(
            flops=12_000_000_000, bytes_accessed=5_000_000, transcendentals=2048
        ),
        name="scan",
    )(lengths, picks, query, key, value, rates, pool, gain)


def out_kernel(heads_all, wout, out):
    rows, _, span = heads_all.shape
    total = jnp.zeros(out.shape, F32)
    for r in range(rows):
        total += jnp.dot(heads_all[r], wout[:, r].reshape(span, out.shape[1]), preferred_element_type=F32)
    out[...] = total.astype(BF)


def out_project(heads_all, wout):
    rows, tokens, span = heads_all.shape
    width = wout.shape[3]
    return pl.pallas_call(
        out_kernel,
        grid=(tokens // SEQ,),
        in_specs=[
            pl.BlockSpec((rows, SEQ, span), lambda i: (0, i, 0)),
            pl.BlockSpec(wout.shape, lambda i: (0, 0, 0, 0)),
        ],
        out_specs=pl.BlockSpec((SEQ, width), lambda i: (i, 0)),
        out_shape=jax.ShapeDtypeStruct((tokens, width), BF),
        compiler_params=pltpu.CompilerParams(vmem_limit_bytes=VMEM_LIMIT),
        cost_estimate=pl.CostEstimate(
            flops=2 * tokens * rows * span * width, bytes_accessed=5_000_000, transcendentals=0
        ),
        name="out_project",
    )(heads_all, wout)


def col_blocks(weight, cols):
    rows, width = weight.shape
    return weight.reshape(rows, cols, width // cols).transpose(1, 0, 2)


def local(
    tokens,
    in_weight,
    out_weight,
    beta_weight,
    conv_weight,
    conv_prior,
    head_gain,
    state_pool,
    state_index,
    lengths,
    page_table,
):
    row_count = lax.axis_size("row")
    col_count = lax.axis_size("col")
    row_id = lax.axis_index("row")
    span = tokens.shape[1]
    heads = state_index.shape[1]
    prompts = lengths.shape[0]
    depth = in_weight.shape[0]

    trainer_in = in_weight.astype(BF)
    trainer_out = out_weight.astype(BF)
    in_parts = trainer_in.reshape(depth, row_count, -1).transpose(1, 0, 2)
    out_parts = trainer_out.reshape(depth, row_count, -1).transpose(1, 0, 2)
    win, out_rows, server_in, server_out, tokens_all = handover(
        in_parts, out_parts, col_blocks(trainer_in, col_count), col_blocks(trainer_out, col_count), tokens, col_count
    )
    server_in = server_in.reshape(-1, server_in.shape[2])
    server_out = server_out.reshape(-1, server_out.shape[2])
    wout = lax.all_gather(out_rows, "col", axis=0)

    my_beta = lax.dynamic_slice_in_dim(beta_weight, row_id * heads, heads, 1).astype(BF)
    wbeta = jnp.pad(my_beta, ((0, 0), (0, DK - heads)))

    pages_dev = prompts * PAGES_SEQ
    capacity = max(1, 2 * pages_dev // col_count)
    slots = capacity * col_count
    table = lax.all_gather(page_table.reshape(pages_dev, 2), "col", axis=0)
    targets, slot_ids = table[:, :, 0], table[:, :, 1]
    order = jnp.arange(pages_dev, dtype=jnp.int32)
    earlier = (targets[:, :, None] == targets[:, None, :]) & (order[None, :] < order[:, None])
    ranks = jnp.sum(earlier.astype(jnp.int32), axis=2)
    col_id = lax.axis_index("col")
    my_targets = page_table[:, :, 0].reshape(-1)
    my_earlier = (my_targets[:, None] == my_targets[None, :]) & (order[None, :] < order[:, None])
    spots = my_targets * capacity + jnp.sum(my_earlier.astype(jnp.int32), axis=1)
    places = jnp.arange(col_count, dtype=jnp.int32)[:, None] * capacity + ranks
    mine = (targets == col_id)[None] & (slot_ids[None] == order[:, None, None])
    sources = jnp.sum(jnp.where(mine, places[None], 0), axis=(1, 2))

    query, key, value, rates, outgoing = project(
        tokens_all, win, wbeta, conv_weight, conv_prior, lengths, spots, slots
    )
    arrived = lax.all_to_all(outgoing, "col", split_axis=0, concat_axis=0, tiled=True)

    gain = head_gain.reshape(1, -1)
    normed, final_state = scan_all(lengths, state_index, query, key, value, rates, state_pool, gain)
    layer_out = out_project(row_gather(normed, row_count), wout)
    page_cache = jnp.take(arrived, sources, axis=0, mode="clip").transpose(0, 2, 1, 3)
    return (server_in, server_out, layer_out, final_state, page_cache)


def solution(mesh):
    return jax.shard_map(
        local,
        mesh=mesh,
        in_specs=(
            P("col", "row"),
            P(("row", "col"), None),
            P(("row", "col"), None),
            P(),
            P(None, "row"),
            P("col", None, "row"),
            P("row"),
            P("col", "row", None, None),
            P("col", "row"),
            P("col"),
            P("col", None, None),
        ),
        out_specs=(
            P("row", "col"),
            P("row", "col"),
            P("col", "row"),
            P("col", "row", None, None),
            P("col", None, None, "row"),
        ),
        check_vma=False,
    )
```

```python
import functools

import jax
import jax.numpy as jnp
from jax import lax
from jax.experimental import pallas as pl
from jax.experimental.pallas import tpu as pltpu
from jax.sharding import PartitionSpec as P

DK = 128
CONV = 4
SEQ = 512
PAGE = 128
PAGES_SEQ = 4
BF = jnp.bfloat16
F32 = jnp.float32
VMEM_LIMIT = 48 * 1024 * 1024


MESH = pl.DeviceIdType.MESH


def handover_kernel(
    chain, in_parts, in_blocks, out_blocks, tokens, win, server_in, server_out, tokens_all, own, part_send, part_recv, tok_send, tok_recv,
    chain_send, chain_recv, pair_send, pair_recv, block_send, block_recv,
):
    row, col = lax.axis_index("row"), lax.axis_index("col")
    rows, cols = in_parts.shape[0], in_blocks.shape[0]
    place, side = col // 2, col % 2
    twin = row + 1 - 2 * (row % 2)
    across = lax.rem(row + 2, rows)
    partner = col + 1 - 2 * side
    chunks = tok_send.shape[1]
    span = tokens.shape[0] // chunks

    barrier = pltpu.get_barrier_semaphore()
    for d in range(1, rows):
        pl.semaphore_signal(barrier, inc=1, device_id=(lax.rem(row + d, rows), col), device_id_type=MESH)
    for d in range(1, cols):
        pl.semaphore_signal(barrier, inc=1, device_id=(row, lax.rem(col + d, cols)), device_id_type=MESH)
    pl.semaphore_wait(barrier, rows - 1 + cols - 1)

    def remote(src, dst, send, recv, target):
        return pltpu.make_async_remote_copy(
            src_ref=src, dst_ref=dst, send_sem=send, recv_sem=recv, device_id=target, device_id_type=MESH
        )

    part_copies = []
    for d in range(1, rows):
        peer = lax.rem(row + d, rows)
        part_copies.append(
            remote(in_parts.at[peer], win.at[col, row], part_send.at[0, d], part_recv.at[0, d], (peer, col))
        )
    for copy in part_copies:
        copy.start()
    own_copies = [
        pltpu.make_async_copy(in_parts.at[row], win.at[col, row], own.at[0]),
        pltpu.make_async_copy(tokens, tokens_all.at[row], own.at[1]),
        pltpu.make_async_copy(in_blocks.at[col], server_in.at[col], own.at[2]),
        pltpu.make_async_copy(out_blocks.at[col], server_out.at[col], own.at[3]),
    ]
    for copy in own_copies:
        copy.start()

    def chunk(slot, n):
        return tokens_all.at[slot, pl.ds(n * span, span)]

    def token_copy(kind, n):
        mine = tokens.at[pl.ds(n * span, span)]
        src = chunk(across, n) if kind == 2 else mine
        dst = chunk(across if kind == 2 else row, n)
        target = (across, col) if kind == 0 else (twin, col)
        return remote(src, dst, tok_send.at[kind, n], tok_recv.at[kind, n], target)

    for n in range(chunks):
        token_copy(0, n).start()
    for n in range(chunks):
        token_copy(1, n).start()

    def chain_copy(way, s):
        block = col - 2 * s if way == 0 else col + 2 * s
        target = (row, col + 2) if way == 0 else (row, col - 2)
        return remote(
            win.at[block], win.at[block], chain_send.at[way, s], chain_recv.at[way, s], target
        )

    def pair_copy(way, s):
        block = col - 2 * s if way == 0 else col + 2 * s
        return remote(win.at[block], win.at[block], pair_send.at[way, s], pair_recv.at[way, s], (row, partner))

    def held(way, s):
        return place - s >= 0 if way == 0 else place + s < chain

    def goes_on(way):
        return place < chain - 1 if way == 0 else place > 0

    own_copies[0].wait()
    for d in range(1, rows):
        part_copies[d - 1].wait_recv()
    for s in range(chain):
        for way in range(2):

            @pl.when(held(way, s))
            def _():
                if s > 0:
                    chain_copy(way, s - 1).wait_recv()

                @pl.when(goes_on(way))
                def _():
                    chain_copy(way, s).start()

                if s > 0 or way == 0:
                    pair_copy(way, s).start()

        if 0 < s <= chunks:
            token_copy(0, s - 1).wait_recv()
            token_copy(2, s - 1).start()
    block_copies = []
    for d in range(1, cols):
        peer = lax.rem(col + d, cols)
        block_copies.append(
            remote(in_blocks.at[peer], server_in.at[col], block_send.at[0, d], block_recv.at[0, d], (row, peer))
        )
        block_copies.append(
            remote(out_blocks.at[peer], server_out.at[col], block_send.at[1, d], block_recv.at[1, d], (row, peer))
        )
    for copy in block_copies:
        copy.start()
    for n in range(max(0, chain - 1), chunks):
        token_copy(0, n).wait_recv()
        token_copy(2, n).start()
    for n in range(chunks):
        token_copy(1, n).wait_recv()
        token_copy(2, n).wait_recv()
        for kind in range(3):
            token_copy(kind, n).wait_send()
    for d in range(1, rows):
        part_copies[d - 1].wait_send()
    for copy in own_copies[1:]:
        copy.wait()
    for s in range(chain):
        for way in range(2):

            @pl.when(held(way, s))
            def _():
                @pl.when(goes_on(way))
                def _():
                    chain_copy(way, s).wait_send()

                if s > 0 or way == 0:
                    pair_copy(way, s).wait()

    for copy in block_copies:
        copy.wait()


def handover(in_parts, in_blocks, out_blocks, tokens, cols):
    rows, depth, width = in_parts.shape
    chain = cols // 2
    chunks = tokens.shape[0] // SEQ
    dma = pltpu.SemaphoreType.DMA
    anywhere = pl.BlockSpec(memory_space=pl.ANY)
    return pl.pallas_call(
        functools.partial(handover_kernel, chain),
        in_specs=[anywhere] * 4,
        out_specs=[anywhere] * 4,
        out_shape=[
            jax.ShapeDtypeStruct((cols, rows, depth, width), BF),
            jax.ShapeDtypeStruct(in_blocks.shape, BF),
            jax.ShapeDtypeStruct(out_blocks.shape, BF),
            jax.ShapeDtypeStruct((rows,) + tokens.shape, BF),
        ],
        scratch_shapes=[
            dma((4,)),
            dma((2, rows)),
            dma((2, rows)),
            dma((3, chunks)),
            dma((3, chunks)),
            dma((2, chain)),
            dma((2, chain)),
            dma((2, chain)),
            dma((2, chain)),
            dma((2, cols)),
            dma((2, cols)),
        ],
        compiler_params=pltpu.CompilerParams(
            collective_id=0, has_side_effects=True, vmem_limit_bytes=VMEM_LIMIT
        ),
        cost_estimate=pl.CostEstimate(flops=0, bytes_accessed=300_000_000, transcendentals=0),
        name="handover",
    )(in_parts, in_blocks, out_blocks, tokens)


def row_gather_kernel(mine, whole, own, send, recv):
    row, col = lax.axis_index("row"), lax.axis_index("col")
    rows = whole.shape[0]
    twin = row + 1 - 2 * (row % 2)
    across = lax.rem(row + 2, rows)
    chunks = send.shape[1]
    span = mine.shape[0] // chunks

    barrier = pltpu.get_barrier_semaphore()
    for peer in (twin, across):
        pl.semaphore_signal(barrier, inc=1, device_id=(peer, col), device_id_type=MESH)
    pl.semaphore_wait(barrier, 2)

    def copy(kind, n):
        piece = pl.ds(n * span, span)
        slot = across if kind == 2 else row
        return pltpu.make_async_remote_copy(
            src_ref=whole.at[across, piece] if kind == 2 else mine.at[piece],
            dst_ref=whole.at[slot, piece],
            send_sem=send.at[kind, n],
            recv_sem=recv.at[kind, n],
            device_id=(across if kind == 0 else twin, col),
            device_id_type=MESH,
        )

    local_copy = pltpu.make_async_copy(mine, whole.at[row], own)
    for kind in range(2):
        for n in range(chunks):
            copy(kind, n).start()
    local_copy.start()
    for n in range(chunks):
        copy(0, n).wait_recv()
        copy(2, n).start()
    for n in range(chunks):
        copy(0, n).wait_send()
        copy(1, n).wait()
        copy(2, n).wait()
    local_copy.wait()


def row_gather(mine, rows):
    chunks = mine.shape[0] // SEQ
    dma = pltpu.SemaphoreType.DMA
    return pl.pallas_call(
        row_gather_kernel,
        in_specs=[pl.BlockSpec(memory_space=pl.ANY)],
        out_specs=pl.BlockSpec(memory_space=pl.ANY),
        out_shape=jax.ShapeDtypeStruct((rows,) + mine.shape, BF),
        scratch_shapes=[dma(()), dma((3, chunks)), dma((3, chunks))],
        compiler_params=pltpu.CompilerParams(
            collective_id=1, has_side_effects=True, vmem_limit_bytes=VMEM_LIMIT
        ),
        cost_estimate=pl.CostEstimate(flops=0, bytes_accessed=100_000_000, transcendentals=0),
        name="row_gather",
    )(mine)


def project_kernel(
    lens, spots, tok, win, wbeta, taps, prior, q_out, k_out, v_out, rates_out, outgoing, line, kv, features, weights, sems
):
    prompt, head = pl.program_id(0), pl.program_id(1)
    heads = pl.num_programs(1)
    rows = tok.shape[0]
    span = tok.shape[2]
    live = lax.broadcasted_iota(jnp.int32, (SEQ, 1), 0) < lens[prompt]

    @pl.when(head == 0)
    def _():
        for r in range(rows):
            features[:, r * span : (r + 1) * span] = tok[r]
        logits = jnp.dot(features[...], wbeta[...], preferred_element_type=F32)
        rates_out[...] = jnp.where(live, jax.nn.sigmoid(logits), 0.0)

    for r in range(rows):
        weights[r * span : (r + 1) * span, :] = win[:, r].reshape(span, 3 * DK)
    total = jnp.dot(features[...], weights[...], preferred_element_type=F32)
    line[5:8, :] = prior[0].astype(F32)
    line[8:, :] = total
    mixed = taps[0:1, :] * line[5 : 5 + SEQ, :]
    for i in range(1, CONV):
        mixed += taps[i : i + 1, :] * line[5 + i : 5 + i + SEQ, :]
    active = mixed * jax.nn.sigmoid(mixed)
    query, key, value = active[:, :DK], active[:, DK : 2 * DK], active[:, 2 * DK :]
    query = query * lax.rsqrt(jnp.sum(query * query, axis=1, keepdims=True) + 1e-06)
    key = key * lax.rsqrt(jnp.sum(key * key, axis=1, keepdims=True) + 1e-06)
    key = jnp.where(live, key, 0.0).astype(BF)
    value = jnp.where(live, value, 0.0).astype(BF)
    q_out[...] = query.astype(BF)
    k_out[...] = key
    v_out[...] = value

    def copies(p, h):
        column = pl.ds(pl.multiple_of(h * DK, DK), DK)
        return [
            pltpu.make_async_copy(
                kv.at[j, pl.ds(g * PAGE, PAGE)],
                outgoing.at[spots[p * PAGES_SEQ + g], j, :, column],
                sems.at[j, g],
            )
            for j in range(2)
            for g in range(PAGES_SEQ)
        ]

    step = prompt * heads + head

    @pl.when(step > 0)
    def _():
        for copy in copies(prompt, head):
            copy.wait()

    kv[0] = key
    kv[1] = value
    for copy in copies(prompt, head):
        copy.start()

    @pl.when(step == pl.num_programs(0) * heads - 1)
    def _():
        for copy in copies(prompt, head):
            copy.wait()


def project(tokens_all, win, wbeta, taps, prior, lengths, spots, slots):
    rows, local_tokens, span = tokens_all.shape
    cols, _, depth, _ = win.shape
    width = taps.shape[1]
    heads = width // (3 * DK)
    prompts = local_tokens // SEQ
    flat = jax.ShapeDtypeStruct((local_tokens, heads * DK), BF)
    block = pl.BlockSpec((SEQ, DK), lambda p, h, *_: (p, h))
    return pl.pallas_call(
        project_kernel,
        grid_spec=pltpu.PrefetchScalarGridSpec(
            num_scalar_prefetch=2,
            grid=(prompts, heads),
            in_specs=[
                pl.BlockSpec((rows, SEQ, span), lambda p, h, *_: (0, p, 0)),
                pl.BlockSpec((cols, rows, depth, 3 * DK), lambda p, h, *_: (0, 0, 0, h)),
                pl.BlockSpec((rows * span, DK), lambda p, h, *_: (0, 0)),
                pl.BlockSpec((CONV, 3 * DK), lambda p, h, *_: (0, h)),
                pl.BlockSpec((1, CONV - 1, 3 * DK), lambda p, h, *_: (p, 0, h)),
            ],
            out_specs=[
                block,
                block,
                block,
                pl.BlockSpec((SEQ, DK), lambda p, h, *_: (p, 0)),
                pl.BlockSpec(memory_space=pl.ANY),
            ],
            scratch_shapes=[
                pltpu.VMEM((SEQ + 8, 3 * DK), F32),
                pltpu.VMEM((2, SEQ, DK), BF),
                pltpu.VMEM((SEQ, rows * span), BF),
                pltpu.VMEM((rows * span, 3 * DK), BF),
                pltpu.SemaphoreType.DMA((2, PAGES_SEQ)),
            ],
        ),
        out_shape=[
            flat,
            flat,
            flat,
            jax.ShapeDtypeStruct((local_tokens, DK), F32),
            jax.ShapeDtypeStruct((slots, 2, PAGE, heads * DK), BF),
        ],
        compiler_params=pltpu.CompilerParams(vmem_limit_bytes=VMEM_LIMIT),
        cost_estimate=pl.CostEstimate(
            flops=2 * local_tokens * rows * span * width,
            bytes_accessed=30_000_000,
            transcendentals=local_tokens * width,
        ),
        name="project",
    )(lengths, spots, tokens_all, win, wbeta, taps, prior)


def mm(a, b):
    return jnp.dot(a.astype(BF), b.astype(BF), preferred_element_type=F32)


def mm_nt(a, b):
    return lax.dot_general(a, b, (((1,), (1,)), ((), ())), preferred_element_type=F32)


def mm_tn(a, b):
    return lax.dot_general(a, b, (((0,), (0,)), ((), ())), preferred_element_type=F32)


def scan_kernel(lens, picks, q_ref, k_ref, v_ref, rates, pool, gain, normed, state_out):
    prompt = pl.program_id(0)
    heads = pool.shape[1]
    size = PAGE
    blocks = SEQ // size
    row = lax.broadcasted_iota(jnp.int32, (size, size), 0)
    column = lax.broadcasted_iota(jnp.int32, (size, size), 1)
    lower = row > column
    causal = row >= column
    eye = (row == column).astype(F32)
    items = [(c, h) for c in range(blocks) for h in range(heads)]

    def part(ref, c, h):
        return ref[c * size : (c + 1) * size, h * DK : (h + 1) * DK]

    keys = {i: part(k_ref, *i) for i in items}
    betas = {(c, h): rates[c * size : (c + 1) * size, h : h + 1] for c, h in items}
    system = {
        i: jnp.where(lower, betas[i] * mm_nt(keys[i], keys[i]), 0.0).astype(BF) for i in items
    }
    inverse = {}
    half = 1
    while half < size:
        inside = (row // (2 * half) == column // (2 * half)) & (row // half != column // half)
        for i in items:
            corner = jnp.where(inside, system[i], jnp.zeros((), BF))
            if half == 1:
                inverse[i] = eye - corner.astype(F32)
            else:
                x = inverse[i].astype(BF)
                inverse[i] = inverse[i] - mm(x, mm(corner, x))
        half *= 2
    weighted, corrections, scores = {}, {}, {}
    for i in items:
        x = inverse[i].astype(BF)
        right = jnp.concatenate(
            [(betas[i] * keys[i].astype(F32)).astype(BF), (betas[i] * part(v_ref, *i).astype(F32)).astype(BF)],
            axis=1,
        )
        solved = mm(x, right)
        weighted[i] = solved[:, :DK].astype(BF)
        corrections[i] = solved[:, DK:]
        scores[i] = jnp.where(causal, mm_nt(part(q_ref, *i), keys[i]), 0.0).astype(BF)
    states = [pool[picks[prompt, h], h] for h in range(heads)]
    for c in range(blocks):
        live = (lax.broadcasted_iota(jnp.int32, (size, 1), 0) + c * size) < lens[prompt]
        for h in range(heads):
            i = (c, h)
            both = mm(jnp.concatenate([weighted[i], part(q_ref, *i)], axis=0), states[h])
            corrected = (corrections[i] - both[:size]).astype(BF)
            out = both[size:] + mm(scores[i], corrected)
            states[h] = states[h] + mm_tn(keys[i], corrected)
            out = jnp.where(live, out, 0.0)
            scale = lax.rsqrt(jnp.mean(out * out, axis=1, keepdims=True) + 1e-05)
            normed[c * size : (c + 1) * size, h * DK : (h + 1) * DK] = (
                out * scale * gain[:, h * DK : (h + 1) * DK]
            ).astype(BF)
    for h in range(heads):
        state_out[0, h] = states[h]


def scan_all(lengths, picks, query, key, value, rates, pool, gain):
    heads = pool.shape[1]
    prompts = query.shape[0] // SEQ
    wide = pl.BlockSpec((SEQ, heads * DK), lambda i, *_: (i, 0))
    return pl.pallas_call(
        scan_kernel,
        grid_spec=pltpu.PrefetchScalarGridSpec(
            num_scalar_prefetch=2,
            grid=(prompts,),
            in_specs=[
                wide,
                wide,
                wide,
                pl.BlockSpec((SEQ, DK), lambda i, *_: (i, 0)),
                pl.BlockSpec(pool.shape, lambda i, *_: (0, 0, 0, 0)),
                pl.BlockSpec((1, heads * DK), lambda i, *_: (0, 0)),
            ],
            out_specs=[
                wide,
                pl.BlockSpec((1, heads, DK, DK), lambda i, *_: (i, 0, 0, 0)),
            ],
        ),
        out_shape=[
            jax.ShapeDtypeStruct(query.shape, BF),
            jax.ShapeDtypeStruct((prompts, heads, DK, DK), F32),
        ],
        compiler_params=pltpu.CompilerParams(vmem_limit_bytes=VMEM_LIMIT),
        cost_estimate=pl.CostEstimate(
            flops=12_000_000_000, bytes_accessed=5_000_000, transcendentals=2048
        ),
        name="scan",
    )(lengths, picks, query, key, value, rates, pool, gain)


def out_kernel(heads_all, wout, out):
    rows, _, span = heads_all.shape
    total = jnp.zeros(out.shape, F32)
    for r in range(rows):
        total += jnp.dot(heads_all[r], wout[:, r].reshape(span, out.shape[1]), preferred_element_type=F32)
    out[...] = total.astype(BF)


def out_project(heads_all, wout, skip):
    rows, tokens, span = heads_all.shape
    width = wout.shape[3] - skip
    return pl.pallas_call(
        out_kernel,
        grid=(tokens // SEQ,),
        in_specs=[
            pl.BlockSpec((rows, SEQ, span), lambda i: (0, i, 0)),
            pl.BlockSpec(wout.shape[:3] + (width,), lambda i: (0, 0, 0, skip // width)),
        ],
        out_specs=pl.BlockSpec((SEQ, width), lambda i: (i, 0)),
        out_shape=jax.ShapeDtypeStruct((tokens, width), BF),
        compiler_params=pltpu.CompilerParams(vmem_limit_bytes=VMEM_LIMIT),
        cost_estimate=pl.CostEstimate(
            flops=2 * tokens * rows * span * width, bytes_accessed=5_000_000, transcendentals=0
        ),
        name="out_project",
    )(heads_all, wout)


def col_blocks(weight, cols):
    rows, width = weight.shape
    return weight.reshape(rows, cols, width // cols).transpose(1, 0, 2)


def local(
    tokens,
    in_weight,
    out_weight,
    beta_weight,
    conv_weight,
    conv_prior,
    head_gain,
    state_pool,
    state_index,
    lengths,
    page_table,
):
    row_count = lax.axis_size("row")
    col_count = lax.axis_size("col")
    row_id = lax.axis_index("row")
    span = tokens.shape[1]
    heads = state_index.shape[1]
    prompts = lengths.shape[0]
    depth = in_weight.shape[0]

    trainer_in = in_weight.astype(BF)
    trainer_out = out_weight.astype(BF)
    in_parts = trainer_in.reshape(depth, row_count, -1).transpose(1, 0, 2)
    out_parts = trainer_out.reshape(depth, row_count, -1).transpose(1, 0, 2)
    win, server_in, server_out, tokens_all = handover(
        jnp.concatenate([in_parts, out_parts], axis=2),
        col_blocks(trainer_in, col_count),
        col_blocks(trainer_out, col_count),
        tokens,
        col_count,
    )
    server_in = server_in.reshape(-1, server_in.shape[2])
    server_out = server_out.reshape(-1, server_out.shape[2])

    my_beta = lax.dynamic_slice_in_dim(beta_weight, row_id * heads, heads, 1).astype(BF)
    wbeta = jnp.pad(my_beta, ((0, 0), (0, DK - heads)))

    pages_dev = prompts * PAGES_SEQ
    capacity = max(1, 2 * pages_dev // col_count)
    slots = capacity * col_count
    table = lax.all_gather(page_table.reshape(pages_dev, 2), "col", axis=0)
    table, tokens_all = lax.optimization_barrier((table, tokens_all))
    targets, slot_ids = table[:, :, 0], table[:, :, 1]
    order = jnp.arange(pages_dev, dtype=jnp.int32)
    earlier = (targets[:, :, None] == targets[:, None, :]) & (order[None, :] < order[:, None])
    ranks = jnp.sum(earlier.astype(jnp.int32), axis=2)
    col_id = lax.axis_index("col")
    my_targets = page_table[:, :, 0].reshape(-1)
    my_earlier = (my_targets[:, None] == my_targets[None, :]) & (order[None, :] < order[:, None])
    spots = my_targets * capacity + jnp.sum(my_earlier.astype(jnp.int32), axis=1)
    places = jnp.arange(col_count, dtype=jnp.int32)[:, None] * capacity + ranks
    mine = (targets == col_id)[None] & (slot_ids[None] == order[:, None, None])
    sources = jnp.sum(jnp.where(mine, places[None], 0), axis=(1, 2))

    query, key, value, rates, outgoing = project(
        tokens_all, win, wbeta, conv_weight, conv_prior, lengths, spots, slots
    )
    arrived = lax.all_to_all(outgoing, "col", split_axis=0, concat_axis=0, tiled=True)

    gain = head_gain.reshape(1, -1)
    normed, final_state = scan_all(lengths, state_index, query, key, value, rates, state_pool, gain)
    layer_out = out_project(row_gather(normed, row_count), win, conv_weight.shape[1])
    page_cache = jnp.take(arrived, sources, axis=0, mode="clip").transpose(0, 2, 1, 3)
    return (server_in, server_out, layer_out, final_state, page_cache)


def solution(mesh):
    return jax.shard_map(
        local,
        mesh=mesh,
        in_specs=(
            P("col", "row"),
            P(("row", "col"), None),
            P(("row", "col"), None),
            P(),
            P(None, "row"),
            P("col", None, "row"),
            P("row"),
            P("col", "row", None, None),
            P("col", "row"),
            P("col"),
            P("col", None, None),
        ),
        out_specs=(
            P("row", "col"),
            P("row", "col"),
            P("col", "row"),
            P("col", "row", None, None),
            P("col", None, None, "row"),
        ),
        check_vma=False,
    )
```
